32 devices in a mesh: field: 16 (over z, y, x), batch: 2 (over core).
Axes of the slice: x: 2, y: 2, z: 4, core: 2. Of those that a mesh axis runs over, the one named last changes fastest.
Arguments:
- pooled: bfloat16 [1024, 16, 256], P('batch', 'field'), may hold values from -6 to 6
- counts: int32 [1024, 16], P('batch', 'field'), may hold values from 1 to 16
- w_pairs: bfloat16 [16, 120, 1024], P('field', None, 'batch'), may hold values from -0.125 to 0.125
- bias_terms: bfloat16 [1024], P('batch'), may hold values from -4 to 4
- grad_act: bfloat16 [1024, 1024], P('batch'), may hold values from -6 to 6
Outputs:
- entry_grad: bfloat16 [1024, 16, 256], P('batch', 'field')
- weight_grad: float32 [16, 120, 1024], P('field', None, 'batch')
The draws below stay inside these ranges and needn't reach their ends.
All inputs are finite; a program needn't handle non-finite values.
Results may differ from the reference program's by a relative error of at most 0.014.
Values may be sent and summed in bfloat16 or wider, within the bound.
A program may use at most 64 MiB of HBM per device.

```python
import jax
import jax.numpy as jnp
from jax import lax

B_DEV = 512
K = 16
H = 1024
FIELDS = 16
SAMPLES = 1024


def plant(values, key, low, largest):
    spot = [jax.random.randint(jax.random.fold_in(key, axis), (), 0, length) for axis, length in enumerate(values.shape)]
    widest = values.shape.index(max(values.shape))
    beside = spot[:widest] + [(spot[widest] + 1) % values.shape[widest]] + spot[widest + 1:]
    return values.at[tuple(spot)].set(low).at[tuple(beside)].set(largest)


def levels(own_key, extent, split, low, largest):
    loudness, own = 1.0, jax.random.fold_in(own_key, 6)
    for position, parts in split:
        draws = jnp.exp(jax.random.uniform(jax.random.fold_in(own, position), (parts,), jnp.float32, low / len(split), largest / len(split)))
        loudness = loudness * jnp.repeat(draws, extent[position] // parts).reshape([-1 if axis == position else 1 for axis in range(len(extent))])
    return loudness


def scatter_about(key, dims, deviation, limit, split=(), held_as=jnp.bfloat16):
    entries = jax.random.normal(key, dims, jnp.float32) * deviation
    if len(split) > 0:
        entries = levels(key, dims, split, -0.22, 0.18) * entries
    return jnp.clip(entries, min=-limit, max=limit).astype(held_as)


def setup_inputs(seed: int = 0) -> dict:
    splits = jax.random.split(jax.random.key(seed), 6)
    return {
        "pooled": scatter_about(splits[0], (SAMPLES, FIELDS, FIELDS * K), 1.0, 6.0, ((0, 2), (1, 16))),
        "counts": plant(jax.random.randint(splits[1], (SAMPLES, FIELDS), 1, 17), jax.random.fold_in(splits[1], 1), 1, 16).astype(jnp.int32),
        "w_pairs": scatter_about(splits[2], (FIELDS, (FIELDS - 1) * (K // 2), H), (FIELDS * (FIELDS - 1) * (K // 2)) ** -0.5, 0.125, ((0, 16), (2, 2))),
        "bias_terms": scatter_about(splits[3], (H,), 1.0, 4.0, ((0, 2),)),
        "grad_act": scatter_about(splits[4], (SAMPLES, H), 1.0, 6.0, ((0, 2),)),
    }


def reference(pooled, counts, w_pairs, bias_terms, grad_act):
    half_depth = K // 2
    own_field = jnp.broadcast_to(jnp.arange(FIELDS, dtype=jnp.int32)[:, None], (FIELDS, FIELDS - 1))
    slot_index = jnp.broadcast_to(jnp.arange(FIELDS - 1, dtype=jnp.int32)[None, :], (FIELDS, FIELDS - 1))
    upper_half = slot_index < own_field
    partner = slot_index + (slot_index >= own_field).astype(jnp.int32)
    weights = w_pairs.astype(jnp.float32)
    bias_wide = bias_terms.astype(jnp.float32)
    sample_rows = B_DEV
    blocks_count = pooled.shape[0] // sample_rows

    def owned_half(tensor):
        picked = tensor[:, own_field, partner, :]
        return jnp.where(upper_half[None, :, :, None], picked[..., half_depth:], picked[..., :half_depth])

    def sample_block(weight_total, inputs):
        pooled_block, count_block, grad_block = inputs
        embedded = pooled_block.astype(jnp.float32).reshape(sample_rows, FIELDS, FIELDS, K)
        flipped = jnp.swapaxes(embedded, 1, 2)
        products = (owned_half(embedded) * owned_half(flipped)).astype(jnp.bfloat16)
        pair_rows = products.astype(jnp.float32).reshape(sample_rows, FIELDS, (FIELDS - 1) * half_depth)
        hidden = jnp.einsum('rip,iph->rh', pair_rows, weights) + bias_wide
        gate_value = jax.nn.sigmoid(hidden)
        slope_act = (grad_block.astype(jnp.float32) * gate_value * (1.0 + hidden * (1.0 - gate_value))).astype(jnp.bfloat16)
        slope_wide = slope_act.astype(jnp.float32)
        pair_grad = jnp.einsum('rh,iph->rip', slope_wide, weights).reshape(sample_rows, FIELDS, FIELDS - 1, half_depth)
        weight_total = weight_total + jnp.einsum('rip,rh->iph', pair_rows, slope_wide)
        zero_half = jnp.zeros_like(pair_grad)
        placed = jnp.where(upper_half[None, :, :, None], jnp.concatenate([zero_half, pair_grad], -1), jnp.concatenate([pair_grad, zero_half], -1))
        dense_grad = jnp.zeros((sample_rows, FIELDS, FIELDS, K), jnp.float32).at[:, own_field, partner, :].set(placed)
        local_part = dense_grad * flipped
        partner_part = lax.optimization_barrier((jnp.swapaxes(dense_grad, 1, 2) * flipped).astype(jnp.bfloat16))
        block_grad = local_part + partner_part.astype(jnp.float32)
        block_grad = block_grad / jnp.sqrt(count_block.astype(jnp.float32))[:, :, None, None]
        return (weight_total, block_grad.reshape(sample_rows, FIELDS, FIELDS * K).astype(jnp.bfloat16))
    weight_start = jnp.zeros((FIELDS, (FIELDS - 1) * half_depth, H), jnp.float32)
    stacked = (pooled.reshape(blocks_count, sample_rows, FIELDS, FIELDS * K), counts.reshape(blocks_count, sample_rows, FIELDS), grad_act.reshape(blocks_count, sample_rows, H))
    weight_total, entry_grads = lax.scan(sample_block, weight_start, stacked)
    return (entry_grads.reshape(pooled.shape[0], FIELDS, FIELDS * K), weight_total)
```

```python
import functools

import jax
import jax.numpy as jnp
from jax import lax
from jax.experimental import pallas as pl
from jax.experimental.pallas import tpu as pltpu
from jax.sharding import PartitionSpec as P

MESH = pl.DeviceIdType.MESH
F32 = jnp.float32
BF16 = jnp.bfloat16


def fold_rows(x, parts):
    if parts == 1:
        return x
    width = x.shape[2] // parts
    return jnp.concatenate([x[:, :, p * width:(p + 1) * width] for p in range(parts)], axis=1)


def unfold_rows(x, parts):
    if parts == 1:
        return x
    height = x.shape[1] // parts
    return jnp.concatenate([x[:, p * height:(p + 1) * height, :] for p in range(parts)], axis=2)


def kernel(fields, shards, fold, e_ref, cnt_ref, w_ref, b_ref, g_hbm, eg_ref, wg_ref,
           out1, in1, mine_v, rec_v, w_all, pairs_t, pairs, send2, in2, acc, g_blk,
           slope_all, out3, in3, wg_out, wg_in, wg_acc,
           s1, r1, sw, rw, s2, r2, sg, rg, s3, r3, sx, rx, sl):
    f = lax.axis_index("field")
    c = lax.axis_index("batch")
    samples = e_ref.shape[0]
    hid = g_hbm.shape[2]
    rows = samples // fields
    part = w_ref.shape[1]
    half = 8
    pair_count = fields * half

    barrier = pltpu.get_barrier_semaphore()

    def greet(d, carry):
        pl.semaphore_signal(barrier, inc=1, device_id={"field": lax.rem(f + d, fields)}, device_id_type=MESH)
        return carry

    def greet_batch(d, carry):
        pl.semaphore_signal(barrier, inc=1, device_id={"batch": lax.rem(c + d, shards)}, device_id_type=MESH)
        return carry

    lax.fori_loop(1, fields, greet, 0)
    lax.fori_loop(1, shards, greet_batch, 0)

    g_copy = pltpu.make_async_copy(g_hbm.at[f], g_blk, sl)
    g_copy.start()

    e_t = e_ref[...].astype(F32).T.reshape(fields, 2 * half, samples)
    block = lax.broadcasted_iota(jnp.int32, (fields, half, samples), 0)
    below = block < f
    low, high = e_t[:, :half, :], e_t[:, half:, :]
    mine_v[...] = jnp.where(below, high, low)
    out1[...] = fold_rows(jnp.where(below, low, high), 2).astype(BF16)
    blank = jnp.zeros((1,) + in1.shape[1:], BF16)
    in1[pl.ds(f, 1)] = blank
    in3[pl.ds(f, 1)] = blank

    w_slots = w_ref[...].astype(F32).reshape(fields - 1, half, part)
    gap = jnp.zeros((1, half, part), F32)
    w_block = lax.broadcasted_iota(jnp.int32, (fields, half, part), 0)
    w_wide = jnp.where(
        w_block < f,
        jnp.concatenate([w_slots, gap], 0),
        jnp.where(w_block > f, jnp.concatenate([gap, w_slots], 0), 0.0),
    )
    bias = jnp.broadcast_to(b_ref[...].astype(F32), (16, part))
    w_all[c] = jnp.concatenate([w_wide.reshape(pair_count, part), bias], 0).astype(BF16)

    pl.semaphore_wait(barrier, fields - 1 + shards - 1)

    def copy1(d):
        to = lax.rem(f + d, fields)
        return pltpu.make_async_remote_copy(
            out1.at[to], in1.at[f], s1.at[d], r1.at[d], device_id={"field": to}, device_id_type=MESH)

    def copyw(d):
        return pltpu.make_async_remote_copy(
            w_all.at[c], w_all.at[c], sw.at[d], rw.at[d],
            device_id={"batch": lax.rem(c + d, shards)}, device_id_type=MESH)

    def copy2(d):
        to = lax.rem(f + d, fields)
        return pltpu.make_async_remote_copy(
            send2.at[to], in2.at[f], s2.at[d], r2.at[d], device_id={"field": to}, device_id_type=MESH)

    def copyg(d):
        to = lax.rem(f + d, fields)
        return pltpu.make_async_remote_copy(
            slope_all.at[f], slope_all.at[f], sg.at[d], rg.at[d], device_id={"field": to}, device_id_type=MESH)

    def copy3(d):
        to = lax.rem(f + d, fields)
        return pltpu.make_async_remote_copy(
            out3.at[to], in3.at[f], s3.at[d], r3.at[d], device_id={"field": to}, device_id_type=MESH)

    def copyx(d):
        to = lax.rem(c + d, shards)
        return pltpu.make_async_remote_copy(
            wg_out.at[to], wg_in.at[c], sx.at[d], rx.at[d], device_id={"batch": to}, device_id_type=MESH)

    def each(count, copy, action):
        def step(d, carry):
            action(copy(d))
            return carry
        lax.fori_loop(1, count, step, 0)

    def wait_in(copy):
        copy.wait_recv()

    def wait_out(copy):
        copy.wait_send()

    def go(copy):
        copy.start()

    each(fields, copy1, go)
    each(shards, copyw, go)
    each(fields, copy1, wait_in)
    received = unfold_rows(in1[...].astype(F32), 2)
    rec_v[...] = received
    product = (mine_v[...] * received).reshape(pair_count, samples)
    pairs_t[...] = product.astype(BF16)
    pairs[...] = product.T.astype(BF16)
    each(shards, copyw, wait_in)

    weights = jnp.concatenate([w_all[s, :pair_count, :] for s in range(shards)], axis=1)
    chunks = 4
    per = fields // chunks

    def hidden_chunk(q, carry):
        lhs = pairs[pl.ds(pl.multiple_of(q * (per * rows), per * rows), per * rows), :]
        part_hidden = jnp.dot(lhs, weights, preferred_element_type=F32).reshape(per, rows, hid)
        send2[pl.ds(q * per, per)] = fold_rows(part_hidden, fold).astype(BF16)
        return carry

    lax.fori_loop(0, chunks, hidden_chunk, 0)
    each(fields, copy2, go)
    in2[f] = send2[f]
    each(fields, copy2, wait_in)

    acc[...] = in2[0].astype(F32)

    def add(j, carry):
        acc[...] += in2[j].astype(F32)
        return carry

    lax.fori_loop(1, fields, add, 0)
    g_copy.wait()
    bias_all = jnp.concatenate([w_all[s, pair_count:, :][:1].astype(F32) for s in range(shards)], axis=1)
    hidden = unfold_rows(acc[...][None], fold)[0] + bias_all
    gate = jax.nn.sigmoid(hidden)
    slope = g_blk[...].astype(F32) * gate * (1.0 + hidden * (1.0 - gate))
    slope_all[f] = fold_rows(slope[None], fold)[0].astype(BF16)
    each(fields, copyg, go)
    each(fields, copyg, wait_in)

    if fold == 1:
        slope_full = slope_all[...].reshape(samples, hid)
    else:
        slope_full = unfold_rows(slope_all[...].astype(F32), fold).reshape(samples, hid).astype(BF16)
    grad_t = lax.dot_general(weights, slope_full, (((1,), (1,)), ((), ())), preferred_element_type=F32)
    grad_t = grad_t.reshape(fields, half, samples)
    out3[...] = fold_rows(grad_t * mine_v[...], 2).astype(BF16)
    each(fields, copy3, go)
    rec_v[...] = grad_t * rec_v[...]

    term = jnp.dot(pairs_t[...], slope_full, preferred_element_type=F32)
    for s in range(shards):
        wg_acc[s] = term[:, s * part:(s + 1) * part]
    wg_out[...] = wg_acc[...].astype(BF16)
    each(shards, copyx, go)

    scale = 1.0 / jnp.sqrt(cnt_ref[...].astype(F32))
    each(fields, copy3, wait_in)
    back = unfold_rows(in3[...].astype(F32), 2) * scale[None]
    local = rec_v[...] * scale[None]
    full = jnp.concatenate([jnp.where(below, back, local), jnp.where(below, local, back)], axis=1)
    eg_ref[...] = full.reshape(fields * 2 * half, samples).T.astype(BF16)

    each(shards, copyx, wait_in)
    wg_out_sum = wg_acc[c]

    def add_wg(d, total):
        return total + wg_in[lax.rem(c + d, shards)].astype(F32)

    for d in range(1, shards):
        wg_out_sum = add_wg(d, wg_out_sum)
    wg3 = wg_out_sum.reshape(fields, half, part)
    slot = lax.broadcasted_iota(jnp.int32, (fields - 1, half, part), 0)
    wg_ref[...] = jnp.where(slot < f, wg3[:-1], wg3[1:]).reshape(pair_count - half, part)

    for count, copy in ((fields, copy1), (shards, copyw), (fields, copy2), (fields, copyg),
                        (fields, copy3), (shards, copyx)):
        each(count, copy, wait_out)


def body(pooled, counts, w_pairs, bias_terms, grad_act):
    fields = lax.axis_size("field")
    shards = lax.axis_size("batch")
    samples = pooled.shape[0]
    width = pooled.shape[2]
    part = w_pairs.shape[2]
    hid = grad_act.shape[1]
    half = width // fields // 2
    rows = samples // fields
    fold = max(1, 16 // rows)
    pair_count = fields * half
    packed = (fields, 2 * half, samples // 2)
    block = (fields, rows * fold, hid // fold)
    vmem = pl.BlockSpec(memory_space=pltpu.VMEM)
    dma = pltpu.SemaphoreType.DMA
    entry, weight = pl.pallas_call(
        functools.partial(kernel, fields, shards, fold),
        out_shape=(
            jax.ShapeDtypeStruct((samples, width), BF16),
            jax.ShapeDtypeStruct((pair_count - half, part), F32),
        ),
        in_specs=[vmem, vmem, vmem, vmem, pl.BlockSpec(memory_space=pl.ANY)],
        out_specs=(vmem, vmem),
        scratch_shapes=[
            pltpu.VMEM(packed, BF16),
            pltpu.VMEM(packed, BF16),
            pltpu.VMEM((fields, half, samples), F32),
            pltpu.VMEM((fields, half, samples), F32),
            pltpu.VMEM((shards, pair_count + 16, part), BF16),
            pltpu.VMEM((pair_count, samples), BF16),
            pltpu.VMEM((samples, pair_count), BF16),
            pltpu.VMEM(block, BF16),
            pltpu.VMEM(block, BF16),
            pltpu.VMEM(block[1:], F32),
            pltpu.VMEM((rows, hid), BF16),
            pltpu.VMEM(block, BF16),
            pltpu.VMEM(packed, BF16),
            pltpu.VMEM(packed, BF16),
            pltpu.VMEM((shards, pair_count, part), BF16),
            pltpu.VMEM((shards, pair_count, part), BF16),
            pltpu.VMEM((shards, pair_count, part), F32),
            dma((fields,)), dma((fields,)), dma((shards,)), dma((shards,)),
            dma((fields,)), dma((fields,)), dma((fields,)), dma((fields,)),
            dma((fields,)), dma((fields,)), dma((shards,)), dma((shards,)), dma,
        ],
        compiler_params=pltpu.CompilerParams(
            collective_id=0, has_side_effects=True, vmem_limit_bytes=48 * 1024 * 1024),
    )(
        pooled.reshape(samples, width),
        counts.reshape(1, samples),
        w_pairs[0],
        bias_terms.reshape(1, part),
        grad_act.reshape(fields, rows, hid),
    )
    return entry.reshape(samples, 1, width), weight[None]


def solution(mesh):
    in_specs = (
        P("batch", "field", None),
        P("batch", "field"),
        P("field", None, "batch"),
        P("batch"),
        P("batch", None),
    )
    out_specs = (P("batch", "field", None), P("field", None, "batch"))
    return jax.shard_map(body, mesh=mesh, in_specs=in_specs, out_specs=out_specs, check_vma=False)
```

```python
import functools

import jax
import jax.numpy as jnp
from jax import lax
from jax.experimental import pallas as pl
from jax.experimental.pallas import tpu as pltpu
from jax.sharding import PartitionSpec as P

MESH = pl.DeviceIdType.MESH
F32 = jnp.float32
BF16 = jnp.bfloat16


def fold_rows(x, parts):
    if parts == 1:
        return x
    width = x.shape[2] // parts
    return jnp.concatenate([x[:, :, p * width:(p + 1) * width] for p in range(parts)], axis=1)


def unfold_rows(x, parts):
    if parts == 1:
        return x
    height = x.shape[1] // parts
    return jnp.concatenate([x[:, p * height:(p + 1) * height, :] for p in range(parts)], axis=2)


def kernel(fields, shards, fold, e_hbm, cnt_ref, w_hbm, b_ref, g_hbm, eg_ref, wg_ref,
           e_ref, w_ref, out1, in1, mine_v, rec_v, w_all, pairs_t, pairs, g_blk,
           keep1, o1, i1, keep2, o2, i2, o3, i3, acc,
           slope_all, out3, in3, wg_out, wg_in, wg_acc,
           s1, r1, sw, rw, s3, r3, sx, rx,
           sa1, ra1, sb1, rb1, sa2, ra2, sb2, rb2, sz3, rz3,
           szg, rzg, sxg, rxg, syg, ryg, sxd, rxd, syd, ryd, sl):
    f = lax.axis_index("field")
    c = lax.axis_index("batch")
    samples = e_ref.shape[0]
    hid = g_hbm.shape[2]
    rows = samples // fields
    part = w_ref.shape[1]
    half = 8
    pair_count = fields * half
    depth = fields // 4
    x = lax.rem(f, 2)
    y = lax.rem(f // 2, 2)
    z = f // 4
    plane = lax.rem(f, 4)
    x_peer = f + 1 - 2 * x
    y_peer = f + 2 - 4 * y

    e_copy = pltpu.make_async_copy(e_hbm, e_ref, sl.at[0])
    w_copy = pltpu.make_async_copy(w_hbm, w_ref, sl.at[1])
    g_copy = pltpu.make_async_copy(g_hbm.at[f], g_blk, sl.at[2])
    e_copy.start()
    w_copy.start()
    g_copy.start()

    barrier = pltpu.get_barrier_semaphore()

    def greet(d, carry):
        pl.semaphore_signal(barrier, inc=1, device_id={"field": lax.rem(f + d, fields)}, device_id_type=MESH)
        return carry

    def greet_batch(d, carry):
        pl.semaphore_signal(barrier, inc=1, device_id={"batch": lax.rem(c + d, shards)}, device_id_type=MESH)
        return carry

    lax.fori_loop(1, fields, greet, 0)
    lax.fori_loop(1, shards, greet_batch, 0)

    e_copy.wait()
    e_t = e_ref[...].astype(F32).T.reshape(fields, 2 * half, samples)
    block = lax.broadcasted_iota(jnp.int32, (fields, half, samples), 0)
    below = block < f
    low, high = e_t[:, :half, :], e_t[:, half:, :]
    mine_v[...] = jnp.where(below, high, low)
    out1[...] = fold_rows(jnp.where(below, low, high), 2).astype(BF16)
    blank = jnp.zeros((1,) + in1.shape[1:], BF16)
    in1[pl.ds(f, 1)] = blank
    in3[pl.ds(f, 1)] = blank

    def copy1(d):
        to = lax.rem(f + d, fields)
        return pltpu.make_async_remote_copy(
            out1.at[to], in1.at[f], s1.at[d], r1.at[d], device_id={"field": to}, device_id_type=MESH)

    def copyw(d):
        return pltpu.make_async_remote_copy(
            w_all.at[c], w_all.at[c], sw.at[d], rw.at[d],
            device_id={"batch": lax.rem(c + d, shards)}, device_id_type=MESH)

    def send(src, dst, s, r, to):
        return pltpu.make_async_remote_copy(
            src, dst, s, r, device_id={"field": to}, device_id_type=MESH)

    def copy_a1(i):
        return send(o1.at[i, 0], i1.at[i, 0], sa1.at[i], ra1.at[i], x_peer)

    def copy_b1(i):
        return send(o1.at[i, 1], i1.at[i, 1], sb1.at[i], rb1.at[i], y_peer)

    def copy_a2(i):
        return send(o2.at[i, 0], i2.at[i, 0], sa2.at[i], ra2.at[i], y_peer)

    def copy_b2(i):
        return send(o2.at[i, 1], i2.at[i, 1], sb2.at[i], rb2.at[i], x_peer)

    def z_peer(d):
        return lax.rem(z + d, depth) * 4 + plane

    def copy_z3(i):
        return send(o3.at[i], i3.at[i], sz3.at[i], rz3.at[i], z_peer(i + 1))

    def copy_zg(d):
        return send(slope_all.at[f], slope_all.at[f], szg.at[d], rzg.at[d], z_peer(d))

    def layer(d):
        return lax.rem(z - d + depth, depth) * 4

    def copy_xg(d):
        at = layer(d) + plane
        return send(slope_all.at[at], slope_all.at[at], sxg.at[d], rxg.at[d], x_peer)

    def copy_yg(d):
        at = layer(d) + plane
        return send(slope_all.at[at], slope_all.at[at], syg.at[d], ryg.at[d], y_peer)

    def copy_xd(d):
        at = layer(d) + (1 - y) * 2 + x
        return send(slope_all.at[at, 0], slope_all.at[at, 0], sxd.at[d], rxd.at[d], x_peer)

    def copy_yd(d):
        at = layer(d) + y * 2 + 1 - x
        return send(slope_all.at[at, 1], slope_all.at[at, 1], syd.at[d], ryd.at[d], y_peer)

    def copy3(d):
        to = lax.rem(f + d, fields)
        return pltpu.make_async_remote_copy(
            out3.at[to], in3.at[f], s3.at[d], r3.at[d], device_id={"field": to}, device_id_type=MESH)

    def copyx(d):
        to = lax.rem(c + d, shards)
        return pltpu.make_async_remote_copy(
            wg_out.at[to], wg_in.at[c], sx.at[d], rx.at[d], device_id={"batch": to}, device_id_type=MESH)

    def each(first, last, copy, action):
        def step(d, carry):
            action(copy(d))
            return carry
        lax.fori_loop(first, last, step, 0)

    def wait_in(copy):
        copy.wait_recv()

    def wait_out(copy):
        copy.wait_send()

    def go(copy):
        copy.start()

    pl.semaphore_wait(barrier, fields - 1 + shards - 1)
    each(1, fields, copy1, go)

    w_copy.wait()
    w_slots = w_ref[...].astype(F32).reshape(fields - 1, half, part)
    gap = jnp.zeros((1, half, part), F32)
    w_block = lax.broadcasted_iota(jnp.int32, (fields, half, part), 0)
    w_wide = jnp.where(
        w_block < f,
        jnp.concatenate([w_slots, gap], 0),
        jnp.where(w_block > f, jnp.concatenate([gap, w_slots], 0), 0.0),
    )
    bias = jnp.broadcast_to(b_ref[...].astype(F32), (16, part))
    w_all[c] = jnp.concatenate([w_wide.reshape(pair_count, part), bias], 0).astype(BF16)
    each(1, shards, copyw, go)

    each(1, fields, copy1, wait_in)
    received = unfold_rows(in1[...].astype(F32), 2)
    rec_v[...] = received
    product = (mine_v[...] * received).reshape(pair_count, samples)
    pairs_t[...] = product.astype(BF16)
    pairs[...] = product.T.astype(BF16)
    each(1, shards, copyw, wait_in)

    weights = jnp.concatenate([w_all[s, :pair_count, :] for s in range(shards)], axis=1)

    def split_columns(t):
        return [fold_rows(t[:, :, p * (hid // 2):(p + 1) * (hid // 2)], fold) for p in range(2)]

    def pick(which, first, second):
        return jnp.where(which == 0, first, second)

    def stage1(i, carry):
        at = lax.rem(z + i + 1, depth) * (4 * rows)
        lhs = pairs[pl.ds(pl.multiple_of(at, 4 * rows), 4 * rows), :]
        t = jnp.dot(lhs, weights, preferred_element_type=F32).reshape(4, rows, hid)
        ta, tb = split_columns(t)
        ta = ta.reshape((2, 2) + ta.shape[1:])
        tb = tb.reshape((2, 2) + tb.shape[1:])
        keep1[i, 0] = pick(x, ta[:, 0], ta[:, 1])
        o1[i, 0] = pick(x, ta[:, 1], ta[:, 0]).astype(BF16)
        copy_a1(i).start()
        keep1[i, 1] = pick(y, tb[0], tb[1])
        o1[i, 1] = pick(y, tb[1], tb[0]).astype(BF16)
        copy_b1(i).start()
        return carry

    lax.fori_loop(0, depth, stage1, 0)

    def stage2(i, carry):
        copy_a1(i).wait_recv()
        ta = keep1[i, 0] + i1[i, 0].astype(F32)
        keep2[i, 0] = pick(y, ta[0], ta[1])
        o2[i, 0] = pick(y, ta[1], ta[0]).astype(BF16)
        copy_a2(i).start()
        copy_b1(i).wait_recv()
        tb = keep1[i, 1] + i1[i, 1].astype(F32)
        keep2[i, 1] = pick(x, tb[0], tb[1])
        o2[i, 1] = pick(x, tb[1], tb[0]).astype(BF16)
        copy_b2(i).start()
        return carry

    lax.fori_loop(0, depth, stage2, 0)

    def stage3(i, carry):
        copy_a2(i).wait_recv()
        copy_b2(i).wait_recv()
        o3[i] = (keep2[i] + i2[i].astype(F32)).astype(BF16)
        copy_z3(i).start()
        return carry

    lax.fori_loop(0, depth - 1, stage3, 0)
    copy_a2(depth - 1).wait_recv()
    copy_b2(depth - 1).wait_recv()
    acc[...] = keep2[depth - 1] + i2[depth - 1].astype(F32)

    def add(i, carry):
        copy_z3(i).wait_recv()
        acc[...] += i3[i].astype(F32)
        return carry

    lax.fori_loop(0, depth - 1, add, 0)
    g_copy.wait()
    bias_all = jnp.concatenate([w_all[s, pair_count:, :][:1].astype(F32) for s in range(shards)], axis=1)
    hidden = jnp.concatenate([unfold_rows(acc[p][None], fold)[0] for p in range(2)], axis=1) + bias_all
    gate = jax.nn.sigmoid(hidden)
    slope = g_blk[...].astype(F32) * gate * (1.0 + hidden * (1.0 - gate))
    slope_a, slope_b = split_columns(slope[None])
    slope_all[f] = jnp.concatenate([slope_a, slope_b], 0).astype(BF16)

    each(1, depth, copy_zg, go)
    copy_xg(0).start()
    copy_yg(0).start()

    def spread(d, carry):
        copy_zg(d).wait_recv()
        copy_xg(d).start()
        copy_yg(d).start()
        return carry

    lax.fori_loop(1, depth, spread, 0)

    def diagonal(d, carry):
        copy_yg(d).wait_recv()
        copy_xd(d).start()
        copy_xg(d).wait_recv()
        copy_yd(d).start()
        return carry

    lax.fori_loop(0, depth, diagonal, 0)
    each(0, depth, copy_xd, wait_in)
    each(0, depth, copy_yd, wait_in)

    if fold == 1:
        halves = [slope_all[:, p].reshape(samples, hid // 2) for p in range(2)]
    else:
        halves = [
            unfold_rows(slope_all[:, p].astype(F32), fold).reshape(samples, hid // 2).astype(BF16)
            for p in range(2)
        ]
    slope_full = jnp.concatenate(halves, axis=1)
    grad_t = lax.dot_general(weights, slope_full, (((1,), (1,)), ((), ())), preferred_element_type=F32)
    grad_t = grad_t.reshape(fields, half, samples)
    out3[...] = fold_rows(grad_t * mine_v[...], 2).astype(BF16)
    each(1, fields, copy3, go)
    rec_v[...] = grad_t * rec_v[...]

    term = jnp.dot(pairs_t[...], slope_full, preferred_element_type=F32)
    for s in range(shards):
        wg_acc[s] = term[:, s * part:(s + 1) * part]
    wg_out[...] = wg_acc[...].astype(BF16)
    each(1, shards, copyx, go)

    scale = 1.0 / jnp.sqrt(cnt_ref[...].astype(F32))
    each(1, fields, copy3, wait_in)
    back = unfold_rows(in3[...].astype(F32), 2) * scale[None]
    local = rec_v[...] * scale[None]
    full = jnp.concatenate([jnp.where(below, back, local), jnp.where(below, local, back)], axis=1)
    eg_ref[...] = full.reshape(fields * 2 * half, samples).T.astype(BF16)

    each(1, shards, copyx, wait_in)
    total = wg_acc[c]
    for d in range(1, shards):
        total = total + wg_in[lax.rem(c + d, shards)].astype(F32)
    wg3 = total.reshape(fields, half, part)
    slot = lax.broadcasted_iota(jnp.int32, (fields - 1, half, part), 0)
    wg_ref[...] = jnp.where(slot < f, wg3[:-1], wg3[1:]).reshape(pair_count - half, part)

    for first, last, copy in (
            (1, fields, copy1), (1, shards, copyw), (0, depth, copy_a1), (0, depth, copy_b1),
            (0, depth, copy_a2), (0, depth, copy_b2), (0, depth - 1, copy_z3), (1, depth, copy_zg),
            (0, depth, copy_xg), (0, depth, copy_yg), (0, depth, copy_xd), (0, depth, copy_yd),
            (1, fields, copy3), (1, shards, copyx)):
        each(first, last, copy, wait_out)


def body(pooled, counts, w_pairs, bias_terms, grad_act):
    fields = lax.axis_size("field")
    shards = lax.axis_size("batch")
    samples = pooled.shape[0]
    width = pooled.shape[2]
    part = w_pairs.shape[2]
    hid = grad_act.shape[1]
    half = width // fields // 2
    rows = samples // fields
    fold = max(1, 16 // rows)
    pair_count = fields * half
    packed = (fields, 2 * half, samples // 2)
    block = (rows * fold, hid // 2 // fold)
    depth = fields // 4
    vmem = pl.BlockSpec(memory_space=pltpu.VMEM)
    anywhere = pl.BlockSpec(memory_space=pl.ANY)
    dma = pltpu.SemaphoreType.DMA
    entry, weight = pl.pallas_call(
        functools.partial(kernel, fields, shards, fold),
        out_shape=(
            jax.ShapeDtypeStruct((samples, width), BF16),
            jax.ShapeDtypeStruct((pair_count - half, part), F32),
        ),
        in_specs=[anywhere, vmem, anywhere, vmem, anywhere],
        out_specs=(vmem, vmem),
        scratch_shapes=[
            pltpu.VMEM((samples, width), BF16),
            pltpu.VMEM((pair_count - half, part), BF16),
            pltpu.VMEM(packed, BF16),
            pltpu.VMEM(packed, BF16),
            pltpu.VMEM((fields, half, samples), F32),
            pltpu.VMEM((fields, half, samples), F32),
            pltpu.VMEM((shards, pair_count + 16, part), BF16),
            pltpu.VMEM((pair_count, samples), BF16),
            pltpu.VMEM((samples, pair_count), BF16),
            pltpu.VMEM((rows, hid), BF16),
            pltpu.VMEM((depth, 2, 2) + block, F32),
            pltpu.VMEM((depth, 2, 2) + block, BF16),
            pltpu.VMEM((depth, 2, 2) + block, BF16),
            pltpu.VMEM((depth, 2) + block, F32),
            pltpu.VMEM((depth, 2) + block, BF16),
            pltpu.VMEM((depth, 2) + block, BF16),
            pltpu.VMEM((depth, 2) + block, BF16),
            pltpu.VMEM((depth, 2) + block, BF16),
            pltpu.VMEM((2,) + block, F32),
            pltpu.VMEM((fields, 2) + block, BF16),
            pltpu.VMEM(packed, BF16),
            pltpu.VMEM(packed, BF16),
            pltpu.VMEM((shards, pair_count, part), BF16),
            pltpu.VMEM((shards, pair_count, part), BF16),
            pltpu.VMEM((shards, pair_count, part), F32),
            dma((fields,)), dma((fields,)), dma((shards,)), dma((shards,)),
            dma((fields,)), dma((fields,)), dma((shards,)), dma((shards,)),
        ] + [dma((depth,))] * 20 + [dma((3,))],
        compiler_params=pltpu.CompilerParams(
            collective_id=0, has_side_effects=True, vmem_limit_bytes=48 * 1024 * 1024),
    )(
        pooled.reshape(samples, width),
        counts.reshape(1, samples),
        w_pairs[0],
        bias_terms.reshape(1, part),
        grad_act.reshape(fields, rows, hid),
    )
    return entry.reshape(samples, 1, width), weight[None]


def solution(mesh):
    in_specs = (
        P("batch", "field", None),
        P("batch", "field"),
        P("field", None, "batch"),
        P("batch"),
        P("batch", None),
    )
    out_specs = (P("batch", "field", None), P("field", None, "batch"))
    return jax.shard_map(body, mesh=mesh, in_specs=in_specs, out_specs=out_specs, check_vma=False)
```

```python
import functools

import jax
import jax.numpy as jnp
from jax import lax
from jax.experimental import pallas as pl
from jax.experimental.pallas import tpu as pltpu
from jax.sharding import PartitionSpec as P

MESH = pl.DeviceIdType.MESH
F32 = jnp.float32
BF16 = jnp.bfloat16


def fold_rows(x, parts):
    if parts == 1:
        return x
    width = x.shape[2] // parts
    return jnp.concatenate([x[:, :, p * width:(p + 1) * width] for p in range(parts)], axis=1)


def unfold_rows(x, parts):
    if parts == 1:
        return x
    height = x.shape[1] // parts
    return jnp.concatenate([x[:, p * height:(p + 1) * height, :] for p in range(parts)], axis=2)


def kernel(fields, shards, fold, phases, e_hbm, cnt_ref, w_hbm, b_ref, g_hbm, eg_ref, wg_ref,
           e_ref, w_ref, out1, in1, mine_v, rec_v, w_all, pairs_t, pairs, g_blk,
           keep1, o1, i1, keep2, o2, i2, o3, i3, acc,
           slope_all, out3, in3, wg_out, wg_in, wg_acc, wg_full, grad_acc,
           s1, r1, sw, rw, s3, r3, sx, rx,
           sa1, ra1, sb1, rb1, sa2, ra2, sb2, rb2, sz3, rz3,
           szg, rzg, sxg, rxg, syg, ryg, sxd, rxd, syd, ryd, sl):
    f = lax.axis_index("field")
    c = lax.axis_index("batch")
    samples = e_ref.shape[0]
    hid = g_hbm.shape[2]
    rows = samples // fields
    part = w_ref.shape[1]
    half = 8
    pair_count = fields * half
    depth = fields // 4
    x = lax.rem(f, 2)
    y = lax.rem(f // 2, 2)
    z = f // 4
    plane = lax.rem(f, 4)
    x_peer = f + 1 - 2 * x
    y_peer = f + 2 - 4 * y

    e_copy = pltpu.make_async_copy(e_hbm, e_ref, sl.at[0])
    w_copy = pltpu.make_async_copy(w_hbm, w_ref, sl.at[1])
    g_copy = pltpu.make_async_copy(g_hbm.at[f], g_blk, sl.at[2])
    e_copy.start()
    w_copy.start()
    g_copy.start()

    barrier = pltpu.get_barrier_semaphore()

    def greet(d, carry):
        pl.semaphore_signal(barrier, inc=1, device_id={"field": lax.rem(f + d, fields)}, device_id_type=MESH)
        return carry

    def greet_batch(d, carry):
        pl.semaphore_signal(barrier, inc=1, device_id={"batch": lax.rem(c + d, shards)}, device_id_type=MESH)
        return carry

    lax.fori_loop(1, fields, greet, 0)
    lax.fori_loop(1, shards, greet_batch, 0)

    e_copy.wait()
    e_t = e_ref[...].astype(F32).T.reshape(fields, 2 * half, samples)
    block = lax.broadcasted_iota(jnp.int32, (fields, half, samples), 0)
    below = block < f
    low, high = e_t[:, :half, :], e_t[:, half:, :]
    mine_v[...] = jnp.where(below, high, low)
    out1[...] = fold_rows(jnp.where(below, low, high), 2).astype(BF16)
    blank = jnp.zeros((1,) + in1.shape[1:], BF16)
    in1[pl.ds(f, 1)] = blank
    in3[pl.ds(f, 1)] = blank

    def copy1(d):
        to = lax.rem(f + d, fields)
        return pltpu.make_async_remote_copy(
            out1.at[to], in1.at[f], s1.at[d], r1.at[d], device_id={"field": to}, device_id_type=MESH)

    def copyw(d):
        return pltpu.make_async_remote_copy(
            w_all.at[c], w_all.at[c], sw.at[d], rw.at[d],
            device_id={"batch": lax.rem(c + d, shards)}, device_id_type=MESH)

    def send(src, dst, s, r, to):
        return pltpu.make_async_remote_copy(
            src, dst, s, r, device_id={"field": to}, device_id_type=MESH)

    def copy_a1(p, i):
        return send(o1.at[p, i, 0], i1.at[p, i, 0], sa1.at[p, i], ra1.at[p, i], x_peer)

    def copy_b1(p, i):
        return send(o1.at[p, i, 1], i1.at[p, i, 1], sb1.at[p, i], rb1.at[p, i], y_peer)

    def copy_a2(p, i):
        return send(o2.at[p, i, 0], i2.at[p, i, 0], sa2.at[p, i], ra2.at[p, i], y_peer)

    def copy_b2(p, i):
        return send(o2.at[p, i, 1], i2.at[p, i, 1], sb2.at[p, i], rb2.at[p, i], x_peer)

    def z_peer(d):
        return lax.rem(z + d, depth) * 4 + plane

    def copy_z3(p, i):
        return send(o3.at[p, i], i3.at[p, i], sz3.at[p, i], rz3.at[p, i], z_peer(i + 1))

    def copy_zg(p, d):
        return send(slope_all.at[f, p], slope_all.at[f, p], szg.at[p, d], rzg.at[p, d], z_peer(d))

    def layer(d):
        return lax.rem(z - d + depth, depth) * 4

    def copy_xg(p, d):
        at = layer(d) + plane
        return send(slope_all.at[at, p], slope_all.at[at, p], sxg.at[p, d], rxg.at[p, d], x_peer)

    def copy_yg(p, d):
        at = layer(d) + plane
        return send(slope_all.at[at, p], slope_all.at[at, p], syg.at[p, d], ryg.at[p, d], y_peer)

    def copy_xd(p, d):
        at = layer(d) + (1 - y) * 2 + x
        return send(slope_all.at[at, p, 0], slope_all.at[at, p, 0], sxd.at[p, d], rxd.at[p, d], x_peer)

    def copy_yd(p, d):
        at = layer(d) + y * 2 + 1 - x
        return send(slope_all.at[at, p, 1], slope_all.at[at, p, 1], syd.at[p, d], ryd.at[p, d], y_peer)

    def copy3(d):
        to = lax.rem(f + d, fields)
        return pltpu.make_async_remote_copy(
            out3.at[to], in3.at[f], s3.at[d], r3.at[d], device_id={"field": to}, device_id_type=MESH)

    def copyx(d):
        to = lax.rem(c + d, shards)
        return pltpu.make_async_remote_copy(
            wg_out.at[to], wg_in.at[c], sx.at[d], rx.at[d], device_id={"batch": to}, device_id_type=MESH)

    def each(first, last, copy, action):
        def step(d, carry):
            action(copy(d))
            return carry
        lax.fori_loop(first, last, step, 0)

    def wait_in(copy):
        copy.wait_recv()

    def wait_out(copy):
        copy.wait_send()

    def go(copy):
        copy.start()

    pl.semaphore_wait(barrier, fields - 1 + shards - 1)
    each(1, fields, copy1, go)

    w_copy.wait()
    w_slots = w_ref[...].astype(F32).reshape(fields - 1, half, part)
    gap = jnp.zeros((1, half, part), F32)
    w_block = lax.broadcasted_iota(jnp.int32, (fields, half, part), 0)
    w_wide = jnp.where(
        w_block < f,
        jnp.concatenate([w_slots, gap], 0),
        jnp.where(w_block > f, jnp.concatenate([gap, w_slots], 0), 0.0),
    )
    bias = jnp.broadcast_to(b_ref[...].astype(F32), (16, part))
    w_all[c] = jnp.concatenate([w_wide.reshape(pair_count, part), bias], 0).astype(BF16)
    each(1, shards, copyw, go)

    each(1, fields, copy1, wait_in)
    received = unfold_rows(in1[...].astype(F32), 2)
    rec_v[...] = received
    product = (mine_v[...] * received).reshape(pair_count, samples)
    pairs_t[...] = product.astype(BF16)
    pairs[...] = product.T.astype(BF16)
    each(1, shards, copyw, wait_in)

    weights = jnp.concatenate([w_all[s, :pair_count, :] for s in range(shards)], axis=1)

    wide = hid // phases

    def split_columns(t):
        return [fold_rows(t[:, :, p * (wide // 2):(p + 1) * (wide // 2)], fold) for p in range(2)]

    def pick(which, first, second):
        return jnp.where(which == 0, first, second)

    def stage1(p):
        def step(i, carry):
            at = lax.rem(z + i + 1, depth) * (4 * rows)
            lhs = pairs[pl.ds(pl.multiple_of(at, 4 * rows), 4 * rows), :]
            t = jnp.dot(lhs, weights[:, p * wide:(p + 1) * wide], preferred_element_type=F32)
            ta, tb = split_columns(t.reshape(4, rows, wide))
            ta = ta.reshape((2, 2) + ta.shape[1:])
            tb = tb.reshape((2, 2) + tb.shape[1:])
            o1[p, i, 0] = pick(x, ta[:, 1], ta[:, 0]).astype(BF16)
            copy_a1(p, i).start()
            o1[p, i, 1] = pick(y, tb[1], tb[0]).astype(BF16)
            copy_b1(p, i).start()
            keep1[p, i, 0] = pick(x, ta[:, 0], ta[:, 1])
            keep1[p, i, 1] = pick(y, tb[0], tb[1])
            return carry

        lax.fori_loop(0, depth, step, 0)

    def stage2(p):
        def step(i, carry):
            copy_a1(p, i).wait_recv()
            ta = keep1[p, i, 0] + i1[p, i, 0].astype(F32)
            o2[p, i, 0] = pick(y, ta[1], ta[0]).astype(BF16)
            copy_a2(p, i).start()
            keep2[p, i, 0] = pick(y, ta[0], ta[1])
            copy_b1(p, i).wait_recv()
            tb = keep1[p, i, 1] + i1[p, i, 1].astype(F32)
            o2[p, i, 1] = pick(x, tb[1], tb[0]).astype(BF16)
            copy_b2(p, i).start()
            keep2[p, i, 1] = pick(x, tb[0], tb[1])
            return carry

        lax.fori_loop(0, depth, step, 0)

    def stage3(p):
        def step(i, carry):
            copy_a2(p, i).wait_recv()
            copy_b2(p, i).wait_recv()
            o3[p, i] = (keep2[p, i] + i2[p, i].astype(F32)).astype(BF16)
            copy_z3(p, i).start()
            return carry

        lax.fori_loop(0, depth - 1, step, 0)
        copy_a2(p, depth - 1).wait_recv()
        copy_b2(p, depth - 1).wait_recv()
        acc[p] = keep2[p, depth - 1] + i2[p, depth - 1].astype(F32)

    bias_all = jnp.concatenate([w_all[s, pair_count:, :][:1].astype(F32) for s in range(shards)], axis=1)

    def activate(p):
        def add(i, carry):
            copy_z3(p, i).wait_recv()
            acc[p] += i3[p, i].astype(F32)
            return carry

        lax.fori_loop(0, depth - 1, add, 0)
        columns = slice(p * wide, (p + 1) * wide)
        hidden = jnp.concatenate([unfold_rows(acc[p, u][None], fold)[0] for u in range(2)], axis=1)
        hidden = hidden + bias_all[:, columns]
        gate = jax.nn.sigmoid(hidden)
        slope = g_blk[:, columns].astype(F32) * gate * (1.0 + hidden * (1.0 - gate))
        slope_a, slope_b = split_columns(slope[None])
        slope_all[f, p] = jnp.concatenate([slope_a, slope_b], 0).astype(BF16)
        each(1, depth, functools.partial(copy_zg, p), go)
        copy_xg(p, 0).start()
        copy_yg(p, 0).start()

    def spread(p):
        def step(d, carry):
            copy_zg(p, d).wait_recv()
            copy_xg(p, d).start()
            copy_yg(p, d).start()
            return carry

        lax.fori_loop(1, depth, step, 0)

    def diagonal(p):
        def step(d, carry):
            copy_yg(p, d).wait_recv()
            copy_xd(p, d).start()
            copy_xg(p, d).wait_recv()
            copy_yd(p, d).start()
            return carry

        lax.fori_loop(0, depth, step, 0)

    def gathered(p):
        each(0, depth, functools.partial(copy_xd, p), wait_in)
        each(0, depth, functools.partial(copy_yd, p), wait_in)
        if fold == 1:
            halves = [slope_all[:, p, u].reshape(samples, wide // 2) for u in range(2)]
        else:
            halves = [
                unfold_rows(slope_all[:, p, u].astype(F32), fold).reshape(samples, wide // 2).astype(BF16)
                for u in range(2)
            ]
        return jnp.concatenate(halves, axis=1)

    def grad_part(p, slope):
        return lax.dot_general(
            weights[:, p * wide:(p + 1) * wide], slope, (((1,), (1,)), ((), ())), preferred_element_type=F32)

    def weight_part(p, slope):
        wg_full[:, p * wide:(p + 1) * wide] = jnp.dot(pairs_t[...], slope, preferred_element_type=F32)

    for stage in (stage1, stage2, stage3):
        for p in range(phases):
            stage(p)
    g_copy.wait()
    for stage in (activate, spread, diagonal):
        for p in range(phases):
            stage(p)

    for p in range(phases):
        slope = gathered(p)
        if p == 0:
            grad_acc[...] = grad_part(p, slope)
        elif p < phases - 1:
            grad_acc[...] += grad_part(p, slope)
        if p < phases - 1:
            weight_part(p, slope)
    grad_t = (grad_acc[...] + grad_part(phases - 1, slope)).reshape(fields, half, samples)
    out3[...] = fold_rows(grad_t * mine_v[...], 2).astype(BF16)
    each(1, fields, copy3, go)
    rec_v[...] = grad_t * rec_v[...]

    weight_part(phases - 1, slope)
    for s in range(shards):
        term = wg_full[:, s * part:(s + 1) * part]
        wg_acc[s] = term
        wg_out[s] = term.astype(BF16)
    each(1, shards, copyx, go)

    scale = 1.0 / jnp.sqrt(cnt_ref[...].astype(F32))
    each(1, fields, copy3, wait_in)
    back = unfold_rows(in3[...].astype(F32), 2) * scale[None]
    local = rec_v[...] * scale[None]
    full = jnp.concatenate([jnp.where(below, back, local), jnp.where(below, local, back)], axis=1)
    eg_ref[...] = full.reshape(fields * 2 * half, samples).T.astype(BF16)

    each(1, shards, copyx, wait_in)
    total = wg_acc[c]
    for d in range(1, shards):
        total = total + wg_in[lax.rem(c + d, shards)].astype(F32)
    wg3 = total.reshape(fields, half, part)
    slot = lax.broadcasted_iota(jnp.int32, (fields - 1, half, part), 0)
    wg_ref[...] = jnp.where(slot < f, wg3[:-1], wg3[1:]).reshape(pair_count - half, part)

    for first, last, copy in (
            (1, fields, copy1), (1, shards, copyw), (1, fields, copy3), (1, shards, copyx)):
        each(first, last, copy, wait_out)
    for p in range(phases):
        for first, last, copy in (
                (0, depth, copy_a1), (0, depth, copy_b1), (0, depth, copy_a2), (0, depth, copy_b2),
                (0, depth - 1, copy_z3), (1, depth, copy_zg), (0, depth, copy_xg), (0, depth, copy_yg),
                (0, depth, copy_xd), (0, depth, copy_yd)):
            each(first, last, functools.partial(copy, p), wait_out)


def body(pooled, counts, w_pairs, bias_terms, grad_act):
    fields = lax.axis_size("field")
    shards = lax.axis_size("batch")
    samples = pooled.shape[0]
    width = pooled.shape[2]
    part = w_pairs.shape[2]
    hid = grad_act.shape[1]
    half = width // fields // 2
    rows = samples // fields
    fold = max(1, 16 // rows)
    pair_count = fields * half
    packed = (fields, 2 * half, samples // 2)
    phases = 2
    block = (rows * fold, hid // phases // 2 // fold)
    depth = fields // 4
    vmem = pl.BlockSpec(memory_space=pltpu.VMEM)
    anywhere = pl.BlockSpec(memory_space=pl.ANY)
    dma = pltpu.SemaphoreType.DMA
    entry, weight = pl.pallas_call(
        functools.partial(kernel, fields, shards, fold, phases),
        out_shape=(
            jax.ShapeDtypeStruct((samples, width), BF16),
            jax.ShapeDtypeStruct((pair_count - half, part), F32),
        ),
        in_specs=[anywhere, vmem, anywhere, vmem, anywhere],
        out_specs=(vmem, vmem),
        scratch_shapes=[
            pltpu.VMEM((samples, width), BF16),
            pltpu.VMEM((pair_count - half, part), BF16),
            pltpu.VMEM(packed, BF16),
            pltpu.VMEM(packed, BF16),
            pltpu.VMEM((fields, half, samples), F32),
            pltpu.VMEM((fields, half, samples), F32),
            pltpu.VMEM((shards, pair_count + 16, part), BF16),
            pltpu.VMEM((pair_count, samples), BF16),
            pltpu.VMEM((samples, pair_count), BF16),
            pltpu.VMEM((rows, hid), BF16),
            pltpu.VMEM((phases, depth, 2, 2) + block, F32),
            pltpu.VMEM((phases, depth, 2, 2) + block, BF16),
            pltpu.VMEM((phases, depth, 2, 2) + block, BF16),
            pltpu.VMEM((phases, depth, 2) + block, F32),
            pltpu.VMEM((phases, depth, 2) + block, BF16),
            pltpu.VMEM((phases, depth, 2) + block, BF16),
            pltpu.VMEM((phases, depth, 2) + block, BF16),
            pltpu.VMEM((phases, depth, 2) + block, BF16),
            pltpu.VMEM((phases, 2) + block, F32),
            pltpu.VMEM((fields, phases, 2) + block, BF16),
            pltpu.VMEM(packed, BF16),
            pltpu.VMEM(packed, BF16),
            pltpu.VMEM((shards, pair_count, part), BF16),
            pltpu.VMEM((shards, pair_count, part), BF16),
            pltpu.VMEM((shards, pair_count, part), F32),
            pltpu.VMEM((pair_count, hid), F32),
            pltpu.VMEM((pair_count, samples), F32),
            dma((fields,)), dma((fields,)), dma((shards,)), dma((shards,)),
            dma((fields,)), dma((fields,)), dma((shards,)), dma((shards,)),
        ] + [dma((phases, depth))] * 20 + [dma((3,))],
        compiler_params=pltpu.CompilerParams(
            collective_id=0, has_side_effects=True, vmem_limit_bytes=48 * 1024 * 1024),
    )(
        pooled.reshape(samples, width),
        counts.reshape(1, samples),
        w_pairs[0],
        bias_terms.reshape(1, part),
        grad_act.reshape(fields, rows, hid),
    )
    return entry.reshape(samples, 1, width), weight[None]


def solution(mesh):
    in_specs = (
        P("batch", "field", None),
        P("batch", "field"),
        P("field", None, "batch"),
        P("batch"),
        P("batch", None),
    )
    out_specs = (P("batch", "field", None), P("field", None, "batch"))
    return jax.shard_map(body, mesh=mesh, in_specs=in_specs, out_specs=out_specs, check_vma=False)
```

```python
import functools

import jax
import jax.numpy as jnp
from jax import lax
from jax.experimental import pallas as pl
from jax.experimental.pallas import tpu as pltpu
from jax.sharding import PartitionSpec as P

MESH = pl.DeviceIdType.MESH
F32 = jnp.float32
BF16 = jnp.bfloat16


def fold_rows(x, parts):
    if parts == 1:
        return x
    width = x.shape[2] // parts
    return jnp.concatenate([x[:, :, p * width:(p + 1) * width] for p in range(parts)], axis=1)


def unfold_rows(x, parts):
    if parts == 1:
        return x
    height = x.shape[1] // parts
    return jnp.concatenate([x[:, p * height:(p + 1) * height, :] for p in range(parts)], axis=2)


def kernel(fields, shards, fold, phases, e_hbm, cnt_ref, w_hbm, b_ref, g_hbm, eg_hbm, wg_hbm,
           e_ref, w_ref, eg_ref, wg_ref, out1, in1, mine_v, rec_v, w_all, pairs_t, pairs, g_blk,
           keep1, o1, i1, keep2, o2, i2, o3, i3, acc,
           slope_all, out3, in3, wg_out, wg_in, wg_acc, wg_full, grad_acc,
           s1, r1, sw, rw, s3, r3, sx, rx,
           sa1, ra1, sb1, rb1, sa2, ra2, sb2, rb2, sz3, rz3,
           szg, rzg, sxg, rxg, syg, ryg, sxd, rxd, syd, ryd, sl):
    f = lax.axis_index("field")
    c = lax.axis_index("batch")
    samples = e_ref.shape[0]
    hid = g_hbm.shape[2]
    rows = samples // fields
    part = w_ref.shape[1]
    half = 8
    pair_count = fields * half
    depth = fields // 4
    x = lax.rem(f, 2)
    y = lax.rem(f // 2, 2)
    z = f // 4
    plane = lax.rem(f, 4)
    x_peer = f + 1 - 2 * x
    y_peer = f + 2 - 4 * y

    e_copy = pltpu.make_async_copy(e_hbm, e_ref, sl.at[0])
    w_copy = pltpu.make_async_copy(w_hbm, w_ref, sl.at[1])
    g_copy = pltpu.make_async_copy(g_hbm.at[f], g_blk, sl.at[2])
    e_copy.start()
    w_copy.start()
    g_copy.start()

    barrier = pltpu.get_barrier_semaphore()

    def greet(d, carry):
        pl.semaphore_signal(barrier, inc=1, device_id={"field": lax.rem(f + d, fields)}, device_id_type=MESH)
        return carry

    def greet_batch(d, carry):
        pl.semaphore_signal(barrier, inc=1, device_id={"batch": lax.rem(c + d, shards)}, device_id_type=MESH)
        return carry

    lax.fori_loop(1, fields, greet, 0)
    lax.fori_loop(1, shards, greet_batch, 0)

    e_copy.wait()
    e_t = e_ref[...].astype(F32).T.reshape(fields, 2 * half, samples)
    block = lax.broadcasted_iota(jnp.int32, (fields, half, samples), 0)
    below = block < f
    low, high = e_t[:, :half, :], e_t[:, half:, :]
    mine_v[...] = jnp.where(below, high, low)
    out1[...] = fold_rows(jnp.where(below, low, high), 2).astype(BF16)
    blank = jnp.zeros((1,) + in1.shape[1:], BF16)
    in1[pl.ds(f, 1)] = blank
    in3[pl.ds(f, 1)] = blank

    def copy1(d):
        to = lax.rem(f + d, fields)
        return pltpu.make_async_remote_copy(
            out1.at[to], in1.at[f], s1.at[d], r1.at[d], device_id={"field": to}, device_id_type=MESH)

    def copyw(d):
        return pltpu.make_async_remote_copy(
            w_all.at[c], w_all.at[c], sw.at[d], rw.at[d],
            device_id={"batch": lax.rem(c + d, shards)}, device_id_type=MESH)

    def send(src, dst, s, r, to):
        return pltpu.make_async_remote_copy(
            src, dst, s, r, device_id={"field": to}, device_id_type=MESH)

    def copy_a1(p, i):
        return send(o1.at[p, i, 0], i1.at[p, i, 0], sa1.at[p, i], ra1.at[p, i], x_peer)

    def copy_b1(p, i):
        return send(o1.at[p, i, 1], i1.at[p, i, 1], sb1.at[p, i], rb1.at[p, i], y_peer)

    def copy_a2(p, i):
        return send(o2.at[p, i, 0], i2.at[p, i, 0], sa2.at[p, i], ra2.at[p, i], y_peer)

    def copy_b2(p, i):
        return send(o2.at[p, i, 1], i2.at[p, i, 1], sb2.at[p, i], rb2.at[p, i], x_peer)

    def z_peer(d):
        return lax.rem(z + d, depth) * 4 + plane

    def copy_z3(p, i):
        return send(o3.at[p, i], i3.at[p, i], sz3.at[p, i], rz3.at[p, i], z_peer(i + 1))

    def copy_zg(p, d):
        return send(slope_all.at[f, p], slope_all.at[f, p], szg.at[p, d], rzg.at[p, d], z_peer(d))

    def layer(d):
        return lax.rem(z - d + depth, depth) * 4

    def copy_xg(p, d):
        at = layer(d) + plane
        return send(slope_all.at[at, p], slope_all.at[at, p], sxg.at[p, d], rxg.at[p, d], x_peer)

    def copy_yg(p, d):
        at = layer(d) + plane
        return send(slope_all.at[at, p], slope_all.at[at, p], syg.at[p, d], ryg.at[p, d], y_peer)

    def copy_xd(p, d):
        at = layer(d) + (1 - y) * 2 + x
        return send(slope_all.at[at, p, 0], slope_all.at[at, p, 0], sxd.at[p, d], rxd.at[p, d], x_peer)

    def copy_yd(p, d):
        at = layer(d) + y * 2 + 1 - x
        return send(slope_all.at[at, p, 1], slope_all.at[at, p, 1], syd.at[p, d], ryd.at[p, d], y_peer)

    def copy3(d):
        to = lax.rem(f + d, fields)
        return pltpu.make_async_remote_copy(
            out3.at[to], in3.at[f], s3.at[d], r3.at[d], device_id={"field": to}, device_id_type=MESH)

    def copyx(d):
        to = lax.rem(c + d, shards)
        return pltpu.make_async_remote_copy(
            wg_out.at[to], wg_in.at[c], sx.at[d], rx.at[d], device_id={"batch": to}, device_id_type=MESH)

    def each(first, last, copy, action):
        def step(d, carry):
            action(copy(d))
            return carry
        lax.fori_loop(first, last, step, 0)

    def wait_in(copy):
        copy.wait_recv()

    def wait_out(copy):
        copy.wait_send()

    def go(copy):
        copy.start()

    pl.semaphore_wait(barrier, fields - 1 + shards - 1)
    each(1, fields, copy1, go)

    w_copy.wait()
    w_slots = w_ref[...].astype(F32).reshape(fields - 1, half, part)
    gap = jnp.zeros((1, half, part), F32)
    w_block = lax.broadcasted_iota(jnp.int32, (fields, half, part), 0)
    w_wide = jnp.where(
        w_block < f,
        jnp.concatenate([w_slots, gap], 0),
        jnp.where(w_block > f, jnp.concatenate([gap, w_slots], 0), 0.0),
    )
    bias = jnp.broadcast_to(b_ref[...].astype(F32), (16, part))
    w_all[c] = jnp.concatenate([w_wide.reshape(pair_count, part), bias], 0).astype(BF16)
    each(1, shards, copyw, go)

    each(1, fields, copy1, wait_in)
    received = unfold_rows(in1[...].astype(F32), 2)
    rec_v[...] = received
    product = (mine_v[...] * received).reshape(pair_count, samples)
    pairs_t[...] = product.astype(BF16)
    pairs[...] = product.T.astype(BF16)
    each(1, shards, copyw, wait_in)

    weights = jnp.concatenate([w_all[s, :pair_count, :] for s in range(shards)], axis=1)

    wide = hid // phases

    def split_columns(t):
        return [fold_rows(t[:, :, p * (wide // 2):(p + 1) * (wide // 2)], fold) for p in range(2)]

    def pick(which, first, second):
        return jnp.where(which == 0, first, second)

    def stage1(p):
        def step(i, carry):
            at = lax.rem(z + i + 1, depth) * (4 * rows)
            lhs = pairs[pl.ds(pl.multiple_of(at, 4 * rows), 4 * rows), :]
            t = jnp.dot(lhs, weights[:, p * wide:(p + 1) * wide], preferred_element_type=F32)
            ta, tb = split_columns(t.reshape(4, rows, wide))
            ta = ta.reshape((2, 2) + ta.shape[1:])
            tb = tb.reshape((2, 2) + tb.shape[1:])
            o1[p, i, 0] = pick(x, ta[:, 1], ta[:, 0]).astype(BF16)
            copy_a1(p, i).start()
            o1[p, i, 1] = pick(y, tb[1], tb[0]).astype(BF16)
            copy_b1(p, i).start()
            keep1[p, i, 0] = pick(x, ta[:, 0], ta[:, 1])
            keep1[p, i, 1] = pick(y, tb[0], tb[1])
            return carry

        lax.fori_loop(0, depth, step, 0)

    def stage2(p):
        def step(i, carry):
            copy_a1(p, i).wait_recv()
            ta = keep1[p, i, 0] + i1[p, i, 0].astype(F32)
            o2[p, i, 0] = pick(y, ta[1], ta[0]).astype(BF16)
            copy_a2(p, i).start()
            keep2[p, i, 0] = pick(y, ta[0], ta[1])
            copy_b1(p, i).wait_recv()
            tb = keep1[p, i, 1] + i1[p, i, 1].astype(F32)
            o2[p, i, 1] = pick(x, tb[1], tb[0]).astype(BF16)
            copy_b2(p, i).start()
            keep2[p, i, 1] = pick(x, tb[0], tb[1])
            return carry

        lax.fori_loop(0, depth, step, 0)

    def stage3(p):
        def step(i, carry):
            copy_a2(p, i).wait_recv()
            copy_b2(p, i).wait_recv()
            o3[p, i] = (keep2[p, i] + i2[p, i].astype(F32)).astype(BF16)
            copy_z3(p, i).start()
            return carry

        lax.fori_loop(0, depth - 1, step, 0)
        copy_a2(p, depth - 1).wait_recv()
        copy_b2(p, depth - 1).wait_recv()
        acc[p] = keep2[p, depth - 1] + i2[p, depth - 1].astype(F32)

    bias_all = jnp.concatenate([w_all[s, pair_count:, :][:1].astype(F32) for s in range(shards)], axis=1)

    def activate(p):
        def add(i, carry):
            copy_z3(p, i).wait_recv()
            acc[p] += i3[p, i].astype(F32)
            return carry

        lax.fori_loop(0, depth - 1, add, 0)
        columns = slice(p * wide, (p + 1) * wide)
        hidden = jnp.concatenate([unfold_rows(acc[p, u][None], fold)[0] for u in range(2)], axis=1)
        hidden = hidden + bias_all[:, columns]
        gate = jax.nn.sigmoid(hidden)
        slope = g_blk[:, columns].astype(F32) * gate * (1.0 + hidden * (1.0 - gate))
        slope_a, slope_b = split_columns(slope[None])
        slope_all[f, p] = jnp.concatenate([slope_a, slope_b], 0).astype(BF16)
        each(1, depth, functools.partial(copy_zg, p), go)
        copy_xg(p, 0).start()
        copy_yg(p, 0).start()

    def spread(p):
        def step(d, carry):
            copy_zg(p, d).wait_recv()
            copy_xg(p, d).start()
            copy_yg(p, d).start()
            return carry

        lax.fori_loop(1, depth, step, 0)

    def diagonal(p):
        def step(d, carry):
            copy_yg(p, d).wait_recv()
            copy_xd(p, d).start()
            copy_xg(p, d).wait_recv()
            copy_yd(p, d).start()
            return carry

        lax.fori_loop(0, depth, step, 0)

    def gathered(p):
        each(0, depth, functools.partial(copy_xd, p), wait_in)
        each(0, depth, functools.partial(copy_yd, p), wait_in)
        if fold == 1:
            halves = [slope_all[:, p, u].reshape(samples, wide // 2) for u in range(2)]
        else:
            halves = [
                unfold_rows(slope_all[:, p, u].astype(F32), fold).reshape(samples, wide // 2).astype(BF16)
                for u in range(2)
            ]
        return jnp.concatenate(halves, axis=1)

    def grad_part(p, slope):
        return lax.dot_general(
            weights[:, p * wide:(p + 1) * wide], slope, (((1,), (1,)), ((), ())), preferred_element_type=F32)

    def weight_part(p, slope):
        wg_full[:, p * wide:(p + 1) * wide] = jnp.dot(pairs_t[...], slope, preferred_element_type=F32)

    for stage in (stage1, stage2, stage3):
        for p in range(phases):
            stage(p)
    g_copy.wait()
    for stage in (activate, spread, diagonal):
        for p in range(phases):
            stage(p)

    for p in range(phases):
        slope = gathered(p)
        if p == 0:
            grad_acc[...] = grad_part(p, slope)
        elif p < phases - 1:
            grad_acc[...] += grad_part(p, slope)
        if p < phases - 1:
            weight_part(p, slope)
    grad_t = (grad_acc[...] + grad_part(phases - 1, slope)).reshape(fields, half, samples)
    out3[...] = fold_rows(grad_t * mine_v[...], 2).astype(BF16)
    each(1, fields, copy3, go)
    rec_v[...] = grad_t * rec_v[...]

    weight_part(phases - 1, slope)
    for s in range(shards):
        term = wg_full[:, s * part:(s + 1) * part]
        wg_acc[s] = term
        wg_out[s] = term.astype(BF16)
    each(1, shards, copyx, go)

    for first, last, copy in ((1, fields, copy1), (1, shards, copyw)):
        each(first, last, copy, wait_out)
    for p in range(phases):
        for first, last, copy in (
                (0, depth, copy_a1), (0, depth, copy_b1), (0, depth, copy_a2), (0, depth, copy_b2),
                (0, depth - 1, copy_z3), (1, depth, copy_zg), (0, depth, copy_xg), (0, depth, copy_yg)):
            each(first, last, functools.partial(copy, p), wait_out)

    each(1, shards, copyx, wait_in)
    total = wg_acc[c]
    for d in range(1, shards):
        total = total + wg_in[lax.rem(c + d, shards)].astype(F32)
    wg3 = total.reshape(fields, half, part)
    slot = lax.broadcasted_iota(jnp.int32, (fields - 1, half, part), 0)
    wg_ref[...] = jnp.where(slot < f, wg3[:-1], wg3[1:]).reshape(pair_count - half, part)
    wg_write = pltpu.make_async_copy(wg_ref, wg_hbm, sl.at[1])
    wg_write.start()
    for p in range(phases):
        each(0, depth, functools.partial(copy_xd, p), wait_out)
        each(0, depth, functools.partial(copy_yd, p), wait_out)

    scale = 1.0 / jnp.sqrt(cnt_ref[...].astype(F32))
    each(1, fields, copy3, wait_in)
    back = unfold_rows(in3[...].astype(F32), 2) * scale[None]
    local = rec_v[...] * scale[None]
    full = jnp.concatenate([jnp.where(below, back, local), jnp.where(below, local, back)], axis=1)
    full = full.reshape(fields * 2 * half, samples)
    mid = samples // 2
    eg_writes = []
    for u in range(2):
        span = pl.ds(u * mid, mid)
        eg_ref[span, :] = full[:, u * mid:(u + 1) * mid].T.astype(BF16)
        eg_writes.append(pltpu.make_async_copy(eg_ref.at[span], eg_hbm.at[span], sl.at[2 * u]))
        eg_writes[-1].start()

    each(1, fields, copy3, wait_out)
    each(1, shards, copyx, wait_out)
    wg_write.wait()
    for write in eg_writes:
        write.wait()


def body(pooled, counts, w_pairs, bias_terms, grad_act):
    fields = lax.axis_size("field")
    shards = lax.axis_size("batch")
    samples = pooled.shape[0]
    width = pooled.shape[2]
    part = w_pairs.shape[2]
    hid = grad_act.shape[1]
    half = width // fields // 2
    rows = samples // fields
    fold = max(1, 16 // rows)
    pair_count = fields * half
    packed = (fields, 2 * half, samples // 2)
    phases = 2
    block = (rows * fold, hid // phases // 2 // fold)
    depth = fields // 4
    vmem = pl.BlockSpec(memory_space=pltpu.VMEM)
    anywhere = pl.BlockSpec(memory_space=pltpu.HBM)
    dma = pltpu.SemaphoreType.DMA
    entry, weight = pl.pallas_call(
        functools.partial(kernel, fields, shards, fold, phases),
        out_shape=(
            jax.ShapeDtypeStruct((samples, width), BF16),
            jax.ShapeDtypeStruct((pair_count - half, part), F32),
        ),
        in_specs=[anywhere, vmem, anywhere, vmem, anywhere],
        out_specs=(anywhere, anywhere),
        scratch_shapes=[
            pltpu.VMEM((samples, width), BF16),
            pltpu.VMEM((pair_count - half, part), BF16),
            pltpu.VMEM((samples, width), BF16),
            pltpu.VMEM((pair_count - half, part), F32),
            pltpu.VMEM(packed, BF16),
            pltpu.VMEM(packed, BF16),
            pltpu.VMEM((fields, half, samples), F32),
            pltpu.VMEM((fields, half, samples), F32),
            pltpu.VMEM((shards, pair_count + 16, part), BF16),
            pltpu.VMEM((pair_count, samples), BF16),
            pltpu.VMEM((samples, pair_count), BF16),
            pltpu.VMEM((rows, hid), BF16),
            pltpu.VMEM((phases, depth, 2, 2) + block, F32),
            pltpu.VMEM((phases, depth, 2, 2) + block, BF16),
            pltpu.VMEM((phases, depth, 2, 2) + block, BF16),
            pltpu.VMEM((phases, depth, 2) + block, F32),
            pltpu.VMEM((phases, depth, 2) + block, BF16),
            pltpu.VMEM((phases, depth, 2) + block, BF16),
            pltpu.VMEM((phases, depth, 2) + block, BF16),
            pltpu.VMEM((phases, depth, 2) + block, BF16),
            pltpu.VMEM((phases, 2) + block, F32),
            pltpu.VMEM((fields, phases, 2) + block, BF16),
            pltpu.VMEM(packed, BF16),
            pltpu.VMEM(packed, BF16),
            pltpu.VMEM((shards, pair_count, part), BF16),
            pltpu.VMEM((shards, pair_count, part), BF16),
            pltpu.VMEM((shards, pair_count, part), F32),
            pltpu.VMEM((pair_count, hid), F32),
            pltpu.VMEM((pair_count, samples), F32),
            dma((fields,)), dma((fields,)), dma((shards,)), dma((shards,)),
            dma((fields,)), dma((fields,)), dma((shards,)), dma((shards,)),
        ] + [dma((phases, depth))] * 20 + [dma((3,))],
        compiler_params=pltpu.CompilerParams(
            collective_id=0, has_side_effects=True, vmem_limit_bytes=60 * 1024 * 1024),
    )(
        pooled.reshape(samples, width),
        counts.reshape(1, samples),
        w_pairs[0],
        bias_terms.reshape(1, part),
        grad_act.reshape(fields, rows, hid),
    )
    return entry.reshape(samples, 1, width), weight[None]


def solution(mesh):
    in_specs = (
        P("batch", "field", None),
        P("batch", "field"),
        P("field", None, "batch"),
        P("batch"),
        P("batch", None),
    )
    out_specs = (P("batch", "field", None), P("field", None, "batch"))
    return jax.shard_map(body, mesh=mesh, in_specs=in_specs, out_specs=out_specs, check_vma=False)
```
